32 devices in a mesh: groups: 2 (over y), row: 16 (over z, x, core).
Axes of the slice: x: 2, y: 2, z: 4, core: 2. Of those that a mesh axis runs over, the one named last changes fastest.
Arguments:
- left_features: bfloat16 [96, 4096], P(('groups', 'row')), parts along dimension 0, may hold values from -24 to 24
- right_features: bfloat16 [96, 4096], P(('groups', 'row')), parts along dimension 0, may hold values from -24 to 24
- alignment_mask: int32 [96, 128], P(('groups', 'row')), parts along dimension 0, may hold values from 0 to 1, as said below
- projection_weight: bfloat16 [1024, 128], replicated, may hold values from -0.1875 to 0.1875
- projection_bias: float32 [128], replicated, may hold values from -6 to 6
- pair_output_cotangent: bfloat16 [96, 48, 128], P(('groups', 'row')), parts along dimension 0, may hold values from -6 to 6
Outputs:
- pair_out: bfloat16 [96, 48, 128], P(('groups', 'row')), parts along dimension 0
- left_feature_gradient: float32 [96, 4096], P(('groups', 'row')), parts along dimension 0
- right_feature_gradient: float32 [96, 4096], P(('groups', 'row')), parts along dimension 0
- grad_weight: float32 [2048, 128], P('groups'), parts along dimension 0
- grad_bias: float32 [256], P('groups'), parts along dimension 0
The draws below stay inside these ranges and needn't reach their ends.
There are 2 independent parts, one for each index of `groups`. The reference program is written for one: setup_inputs(seed, part) draws one part's arguments, and reference() takes and returns one part's arrays. A program takes and returns all parts, laid end to end along the dimension named above; an argument that names none is the same for every part. Nothing has to cross between parts.
Inputs may be any that keep to these rules, and one draw needn't show every extreme that they name: `alignment_mask`: each protein is present up to some length and padded after it: from some residue on to the last, all entries are 0; that length lies between 36 and 47.
All inputs are finite; a program needn't handle non-finite values.
Results may differ from the reference program's by a relative error of at most 0.0041.
Values may be sent and summed in bfloat16 or wider, within the bound.
A program may use at most 128 MiB of HBM per device.

```python
import math
import jax
import jax.numpy as jnp
from jax import lax

ALIGNMENT_ROWS = 128
FEATURE_CHANNELS = 32
PAIR_CHANNELS = 128
RESIDUE_COUNT = 48


def draw_alignment_mask(key, part):
    key_len, random_key_bits = jax.random.split(jax.random.fold_in(key, 17))
    valid_len = jax.random.randint(key_len, (), RESIDUE_COUNT - RESIDUE_COUNT // 4, RESIDUE_COUNT)
    retained_random_bits = jax.random.randint(random_key_bits, (RESIDUE_COUNT, ALIGNMENT_ROWS), 0, 20) < 17
    block_position = lax.broadcasted_iota(jnp.int32, (RESIDUE_COUNT, ALIGNMENT_ROWS), 0)
    return (retained_random_bits & (block_position < valid_len)).astype(jnp.int32)


def strengthened(drawn, key, source, target, parts, factor):
    def block_of(dim):
        return (jnp.arange(drawn.shape[dim]) // (drawn.shape[dim] // parts)).reshape((-1,) + (1,) * (drawn.ndim - 1 - dim))

    near = jax.random.permutation(key, parts)[block_of(target)]
    second = (block_of(target) + parts // 2) % parts
    return jnp.where((block_of(source) == near) | (block_of(source) == second), factor * drawn, drawn)


def block_scale(rng, dims, shards, smallest, largest):
    def one(dim, shards_of):
        draws = jax.random.uniform(jax.random.fold_in(jax.random.fold_in(rng, 6), dim), (shards_of,), jnp.float32, smallest / len(shards), largest / len(shards))
        return jnp.repeat(jnp.exp(draws), dims[dim] // shards_of).reshape((-1,) + (1,) * (len(dims) - dim - 1))

    factor_of = one(*shards[0])
    for cut in shards[1:]:
        factor_of = factor_of * one(*cut)
    return factor_of


def gaussian(own_key, dims, scale, bound, shards=(), kind=jnp.bfloat16):
    result = scale * jax.random.normal(own_key, dims, jnp.float32)
    if shards:
        result = result * block_scale(own_key, dims, shards, -0.22, 0.18)
    return jnp.clip(result, -bound, bound).astype(kind)


def noise_with(stream_key, extent, spread, most, pieces, heavy, held_as=jnp.bfloat16):
    array = spread * jax.random.normal(stream_key, extent, jnp.float32)
    if pieces:
        array = array * block_scale(stream_key, extent, pieces, -0.22, 0.18)
    return jnp.clip(strengthened(array, jax.random.fold_in(stream_key, 3), *heavy), -most, most).astype(held_as)


def setup_inputs(seed: int = 0, part: int = 0) -> dict:
    key_of = jax.random.split(jax.random.key(seed), 7)
    part_keys = jax.random.split(jax.random.fold_in(key_of[6], part), 7)
    return {
        "left_features": gaussian(part_keys[0], (RESIDUE_COUNT, ALIGNMENT_ROWS * FEATURE_CHANNELS), 4.0, 24.0, ((0, 16),)),
        "right_features": gaussian(part_keys[1], (RESIDUE_COUNT, ALIGNMENT_ROWS * FEATURE_CHANNELS), 4.0, 24.0, ((0, 16),)),
        "alignment_mask": draw_alignment_mask(jax.random.fold_in(jax.random.fold_in(key_of[6], part), 71), part),
        "projection_weight": gaussian(key_of[3], (FEATURE_CHANNELS * FEATURE_CHANNELS, PAIR_CHANNELS), (FEATURE_CHANNELS * FEATURE_CHANNELS) ** -0.5, 0.1875),
        "projection_bias": gaussian(key_of[4], (PAIR_CHANNELS,), 1.0, 6.0, (), jnp.float32),
        "pair_output_cotangent": noise_with(part_keys[5], (RESIDUE_COUNT, RESIDUE_COUNT, PAIR_CHANNELS), 1.0, 6.0, ((0, 16),), (0, 1, 16, 2.0)),
    }


def reference(left_features, right_features, alignment_mask, projection_weight, projection_bias, pair_output_cotangent):
    hp = lax.Precision.HIGHEST
    mask_float = alignment_mask.astype(jnp.float32)
    left_masked = left_features.astype(jnp.float32).reshape(RESIDUE_COUNT, ALIGNMENT_ROWS, FEATURE_CHANNELS) * mask_float[:, :, None]
    right_masked = right_features.astype(jnp.float32).reshape(RESIDUE_COUNT, ALIGNMENT_ROWS, FEATURE_CHANNELS) * mask_float[:, :, None]
    counts = jnp.dot(mask_float, mask_float.T, precision=hp)
    pair_norm = jnp.maximum(counts, 1.0)
    rows_per_block = math.gcd(RESIDUE_COUNT, 32)
    number_of_blocks = RESIDUE_COUNT // rows_per_block
    weight_f = projection_weight

    def block_step(state_carry, index):
        right_accumulator, weight_acc, bias_acc = state_carry
        first = index * rows_per_block
        left_blk = lax.dynamic_slice_in_dim(left_masked, first, rows_per_block, 0)
        norm_blk = lax.dynamic_slice_in_dim(pair_norm, first, rows_per_block, 0)[:, :, None]
        cot_blk = lax.dynamic_slice_in_dim(pair_output_cotangent, first, rows_per_block, 0)
        outer_prod = jnp.einsum('isc,jse->ijce', left_blk, right_masked, precision=hp).reshape(rows_per_block, RESIDUE_COUNT, FEATURE_CHANNELS * FEATURE_CHANNELS)
        prob = (outer_prod / norm_blk).astype(jnp.bfloat16)
        flat_prob = prob.reshape(rows_per_block * RESIDUE_COUNT, FEATURE_CHANNELS * FEATURE_CHANNELS)
        cot_flat = cot_blk.reshape(rows_per_block * RESIDUE_COUNT, PAIR_CHANNELS)
        pair_block = (jnp.dot(flat_prob, weight_f, preferred_element_type=jnp.float32) + projection_bias).astype(jnp.bfloat16)
        prob_grad = jnp.dot(cot_flat, weight_f.T, preferred_element_type=jnp.float32).reshape(rows_per_block, RESIDUE_COUNT, FEATURE_CHANNELS * FEATURE_CHANNELS)
        outer_grad = (prob_grad / norm_blk).astype(jnp.bfloat16).astype(jnp.float32).reshape(rows_per_block, RESIDUE_COUNT, FEATURE_CHANNELS, FEATURE_CHANNELS)
        left_grad = jnp.einsum('ijce,jse->isc', outer_grad, right_masked, precision=hp)
        right_accumulator = right_accumulator + jnp.einsum('ijce,isc->jse', outer_grad, left_blk, precision=hp)
        weight_acc = weight_acc + jnp.dot(flat_prob.T, cot_flat, preferred_element_type=jnp.float32)
        bias_acc = bias_acc + jnp.sum(cot_flat.astype(jnp.float32), axis=0)
        return (right_accumulator, weight_acc, bias_acc), (pair_block.reshape(rows_per_block, RESIDUE_COUNT, PAIR_CHANNELS), left_grad)

    starting_carry = (jnp.zeros((RESIDUE_COUNT, ALIGNMENT_ROWS, FEATURE_CHANNELS), jnp.float32), jnp.zeros((FEATURE_CHANNELS * FEATURE_CHANNELS, PAIR_CHANNELS), jnp.float32), jnp.zeros((PAIR_CHANNELS,), jnp.float32))
    (right_accumulator, weight_acc, bias_acc), (pairs, left_gradient_parts) = lax.scan(block_step, starting_carry, jnp.arange(number_of_blocks, dtype=jnp.int32))
    pair_out = pairs.reshape(RESIDUE_COUNT, RESIDUE_COUNT, PAIR_CHANNELS)
    left_feature_gradient = (left_gradient_parts.reshape(RESIDUE_COUNT, ALIGNMENT_ROWS, FEATURE_CHANNELS) * mask_float[:, :, None]).reshape(RESIDUE_COUNT, ALIGNMENT_ROWS * FEATURE_CHANNELS)
    right_feature_gradient = (right_accumulator * mask_float[:, :, None]).reshape(RESIDUE_COUNT, ALIGNMENT_ROWS * FEATURE_CHANNELS)
    return pair_out, left_feature_gradient, right_feature_gradient, weight_acc / RESIDUE_COUNT, bias_acc / RESIDUE_COUNT
```

```python
import functools
import math

import jax
import jax.numpy as jnp
from jax import lax
from jax.experimental import pallas as pl
from jax.experimental.pallas import tpu as pltpu
from jax.sharding import PartitionSpec as P

MESH = pl.DeviceIdType.MESH
NT = (((1,), (1,)), ((), ()))
TN = (((0,), (0,)), ((), ()))


def gather_kernel(levels, pack_ref, out_ref, send_sem, recv_sem, own_sem):
    group = lax.axis_index("groups")
    me = lax.axis_index("row")
    rows = pack_ref.shape[0]
    half_rows = rows // 2
    core = lax.rem(me, 2)
    x = lax.rem(me // 2, 2)
    z = me // 4

    def rank(zz, xx, cc):
        return zz * 4 + xx * 2 + cc

    sib, xn = rank(z, x, 1 - core), rank(z, 1 - x, core)
    up, dn = rank(z + 1, x, core), rank(z - 1, x, core)
    has_up, has_dn = z < levels - 1, z > 0

    barrier = pltpu.get_barrier_semaphore()

    def greet(target):
        pl.semaphore_signal(barrier, inc=1, device_id=(group, target), device_id_type=MESH)

    greet(sib)
    greet(xn)
    pl.when(has_up)(lambda: greet(up))
    pl.when(has_dn)(lambda: greet(dn))
    own = pltpu.make_async_copy(pack_ref, out_ref.at[pl.ds(me * rows, rows)], own_sem)
    own.start()
    pl.semaphore_wait(barrier, 2 + has_up.astype(jnp.int32) + has_dn.astype(jnp.int32))

    pending = []

    def place(owner, half):
        return out_ref.at[pl.ds(owner * rows + half * half_rows, half_rows)]

    def copy_of(owner, half, target, index, local):
        src = pack_ref.at[pl.ds(half * half_rows, half_rows)] if local else place(owner, half)
        return pltpu.make_async_remote_copy(
            src_ref=src,
            dst_ref=place(owner, half),
            send_sem=send_sem.at[index],
            recv_sem=recv_sem.at[owner, half],
            device_id=(group, target),
            device_id_type=MESH,
        )

    def send(owner, half, target, cond=None, local=False):
        copy = copy_of(owner, half, target, len(pending), local)
        pending.append((copy, cond))
        if cond is None:
            copy.start()
        else:
            pl.when(cond)(copy.start)

    def arrive(owner, half, cond=None):
        copy = copy_of(owner, half, sib, 0, False)
        if cond is None:
            copy.wait_recv()
        else:
            pl.when(cond)(copy.wait_recv)

    def both(a, b):
        return a if b is None else jnp.logical_and(a, b)

    send(me, 0, xn, local=True)
    send(me, 1, up, has_up, local=True)
    send(me, 1, dn, has_dn, local=True)
    send(me, 0, up, has_up, local=True)
    send(me, 0, dn, has_dn, local=True)
    send(me, 1, xn, local=True)
    send(me, 0, sib, local=True)
    send(me, 1, sib, local=True)

    arrive(xn, 0)
    send(xn, 0, up, has_up)
    send(xn, 0, dn, has_dn)
    send(xn, 0, sib)

    def from_level(k, sign, xx, half):
        zo = z + sign * k
        cond = zo >= 0 if sign < 0 else zo <= levels - 1
        owner = rank(zo, xx, core)
        arrive(owner, half, cond)
        if half == 0 or xx is x:
            onward, has_onward = (up, has_up) if sign < 0 else (dn, has_dn)
            if k < levels - 1:
                send(owner, half, onward, both(has_onward, cond))
        if half == 1 and xx is x:
            send(owner, half, xn, cond)
        send(owner, half, sib, cond)

    other = 1 - x
    for k in range(1, levels):
        for sign in (-1, 1):
            from_level(k, sign, x, 1)
        for sign in (-1, 1):
            from_level(k, sign, x, 0)
        if k == 1:
            arrive(xn, 1)
            send(xn, 1, sib)
        for sign in (-1, 1):
            from_level(k, sign, other, 0)
        for sign in (-1, 1):
            from_level(k, sign, other, 1)

    for zz in range(levels):
        for xx in range(2):
            for half in range(2):
                arrive(rank(zz, xx, 1 - core), half)
    for copy, cond in pending:
        if cond is None:
            copy.wait_send()
        else:
            pl.when(cond)(copy.wait_send)
    own.wait()


def gather(pack, size):
    levels = size // 4
    rows, lanes = pack.shape
    return pl.pallas_call(
        functools.partial(gather_kernel, levels),
        out_shape=jax.ShapeDtypeStruct((size * rows, lanes), pack.dtype),
        in_specs=[pl.BlockSpec(memory_space=pltpu.VMEM)],
        out_specs=pl.BlockSpec(memory_space=pltpu.VMEM),
        scratch_shapes=[
            pltpu.SemaphoreType.DMA((64,)),
            pltpu.SemaphoreType.DMA((size, 2)),
            pltpu.SemaphoreType.DMA,
        ],
        compiler_params=pltpu.CompilerParams(
            collective_id=0, has_side_effects=True, vmem_limit_bytes=32 * 1024 * 1024
        ),
        name="gather",
    )(pack)


def compute_kernel(
    n, sr, ch, rows, g, w_ref, bias_ref, pair_ref, lg_ref, rg_ref, gw_ref, gb_ref,
    fa, fb, fc, mf, rn, bp, ap, wf, wl, wr, cb, t, acc,
):
    f32, bf16 = jnp.float32, jnp.bfloat16
    me = lax.axis_index("row")
    res = n * sr
    pad = 64
    lane = 128
    hp = ch // 2
    fr = sr * ch
    cot_at, mask_at = 2 * fr, 2 * fr + sr * res

    def dot(a, b, dims=(((1,), (0,)), ((), ()))):
        return lax.dot_general(a, b, dims, preferred_element_type=f32)

    mf[...] = jnp.zeros_like(mf)
    for d in range(n):
        base = d * rows
        fa[d * fr:(d + 1) * fr] = g[base:base + fr].astype(f32)
        fb[d * fr:(d + 1) * fr] = g[base + fr:base + 2 * fr].astype(f32)
        fc[d * sr * res:(d + 1) * sr * res] = g[base + cot_at:base + mask_at].astype(f32)
        m = g[base + mask_at:base + mask_at + 16].astype(f32)[:sr]
        mf[d * sr:(d + 1) * sr] = m
    masks = mf[...].astype(bf16)
    rn[...] = 1.0 / jnp.maximum(dot(masks, jnp.concatenate([masks, masks], 0), NT), 1.0)

    bp[...] = jnp.zeros_like(bp)
    ap[...] = jnp.zeros_like(ap)
    for e in range(ch):
        bp[e * pad:e * pad + res] = fb[pl.ds(e, res, stride=ch), :].astype(bf16)
        ap[e * pad:e * pad + res] = fa[pl.ds(e, res, stride=ch), :].astype(bf16)
    wf[...] = w_ref[...].astype(f32)
    for p in range(hp):
        for h in range(2):
            q = 2 * p + h
            wl[p * ch:(p + 1) * ch, h * lane:(h + 1) * lane] = wf[pl.ds(q, ch, stride=ch), :].astype(bf16)
            wr[p * ch:(p + 1) * ch, h * lane:(h + 1) * lane] = w_ref[q * ch:(q + 1) * ch]

    gb_ref[...] = jnp.sum(fc[...], axis=0, keepdims=True) * (1.0 / res)
    cb[...] = jnp.zeros_like(cb)
    acc[...] = jnp.zeros_like(acc)

    def fill_cot(k, block):
        cb[k * lane:k * lane + res, 0:lane] = block
        cb[k * lane + pad:k * lane + pad + res, lane:2 * lane] = block

    def fill_prob(left, first, count):
        for p in range(0, hp, 2):
            o = dot(left, bp[p * lane:(p + 2) * lane], NT)
            for k in range(count):
                scale = rn[pl.ds(first + k, 1), :]
                for u in range(2):
                    t[(p + u) * ch:(p + u + 1) * ch, k * lane:(k + 1) * lane] = (
                        o[k * ch:(k + 1) * ch, u * lane:(u + 1) * lane] * scale
                    ).astype(bf16)

    def step(v, carry):
        base = pl.multiple_of(v * (2 * rows), 16)
        left = jnp.concatenate([g[pl.ds(base, fr)], g[pl.ds(base + rows, fr)]], 0)
        fill_prob(left, v * (2 * sr), 2 * sr)
        for k in range(2 * sr):
            fill_cot(k, g[pl.ds(base + (k // sr) * rows + cot_at + (k % sr) * res, res)])
        acc[...] += dot(t[...], cb[...])
        return carry

    lax.fori_loop(0, n // 2, step, 0)
    for p in range(hp):
        for h in range(2):
            gw_ref[pl.ds(2 * p + h, ch, stride=ch), :] = (
                acc[p * ch:(p + 1) * ch, h * lane:(h + 1) * lane] * (1.0 / res)
            )

    base = pl.multiple_of(me * rows, 16)
    width = sr * lane
    scales = jnp.concatenate([rn[pl.ds(me * sr + k, 1), :] for k in range(sr)], 1)

    def side(weights, features):
        og = (dot(weights, cb[:width], NT) * scales).astype(bf16)
        flat = jnp.concatenate(
            [
                jnp.concatenate(
                    [og[p * ch:(p + 1) * ch, k * lane:(k + 1) * lane] for p in range(hp)], 1
                )
                for k in range(sr)
            ],
            0,
        )
        return dot(flat, features[...])

    fill_prob(g[pl.ds(base, fr)], me * sr, sr)
    for k in range(sr):
        fill_cot(k, g[pl.ds(base + cot_at + k * res, res)])
    pairs = dot(t[:, :width], wl[...], TN)
    lg = side(wl[...], bp)
    for k in range(sr):
        pair_ref[k * res:(k + 1) * res] = (
            pairs[k * lane:k * lane + res, :lane]
            + pairs[k * lane + pad:k * lane + pad + res, lane:]
            + bias_ref[...]
        ).astype(bf16)
        lg_ref[k * ch:(k + 1) * ch] = lg[k * ch:(k + 1) * ch] * mf[pl.ds(me * sr + k, 1), :]
    for k in range(sr):
        fill_cot(k, fc[pl.ds(me * sr + k, res, stride=res), :].astype(bf16))
    rg = side(wr[...], ap)
    for k in range(sr):
        rg_ref[k * ch:(k + 1) * ch] = rg[k * ch:(k + 1) * ch] * mf[pl.ds(me * sr + k, 1), :]


def compute(g, weight, bias, n, sr, ch, rows):
    f32, bf16 = jnp.float32, jnp.bfloat16
    res, hidden, lane = n * sr, ch * ch, 128
    vmem = pl.BlockSpec(memory_space=pltpu.VMEM)
    return pl.pallas_call(
        functools.partial(compute_kernel, n, sr, ch, rows),
        out_shape=(
            jax.ShapeDtypeStruct((sr * res, lane), bf16),
            jax.ShapeDtypeStruct((sr * ch, lane), f32),
            jax.ShapeDtypeStruct((sr * ch, lane), f32),
            jax.ShapeDtypeStruct((hidden, lane), f32),
            jax.ShapeDtypeStruct((1, lane), f32),
        ),
        in_specs=[vmem] * 3,
        out_specs=(vmem,) * 5,
        scratch_shapes=[
            pltpu.VMEM((res * ch, lane), f32),
            pltpu.VMEM((res * ch, lane), f32),
            pltpu.VMEM((res * res, lane), f32),
            pltpu.VMEM((64, lane), f32),
            pltpu.VMEM((64, lane), f32),
            pltpu.VMEM((ch * 64, lane), bf16),
            pltpu.VMEM((ch * 64, lane), bf16),
            pltpu.VMEM((hidden, lane), f32),
            pltpu.VMEM((hidden // 2, 2 * lane), bf16),
            pltpu.VMEM((hidden // 2, 2 * lane), bf16),
            pltpu.VMEM((2 * sr * lane, 2 * lane), bf16),
            pltpu.VMEM((hidden // 2, 2 * sr * lane), bf16),
            pltpu.VMEM((hidden // 2, 2 * lane), f32),
        ],
        compiler_params=pltpu.CompilerParams(vmem_limit_bytes=40 * 1024 * 1024),
        name="compute",
    )(g, weight, bias)


def gathered_local(
    left_features,
    right_features,
    alignment_mask,
    projection_weight,
    projection_bias,
    pair_output_cotangent,
):
    sr, width = left_features.shape
    depth = alignment_mask.shape[1]
    ch = width // depth
    n = lax.axis_size("row")
    res = n * sr
    mask = alignment_mask.astype(jnp.bfloat16)

    def by_channel(features):
        masked = features.reshape(sr, depth, ch) * mask[:, :, None]
        return masked.transpose(0, 2, 1).reshape(sr * ch, depth)

    parts = [
        by_channel(left_features),
        by_channel(right_features),
        pair_output_cotangent.reshape(sr * res, -1),
        mask,
    ]
    used = sum(part.shape[0] for part in parts)
    rows = -(-used // 32) * 32
    parts.append(jnp.zeros((rows - used, depth), jnp.bfloat16))
    pack = jnp.concatenate(parts, 0)
    pair, lg, rg, gw, gb = compute(
        gather(pack, n), projection_weight, projection_bias.reshape(1, -1), n, sr, ch, rows
    )

    def by_row(grad):
        return grad.reshape(sr, ch, depth).transpose(0, 2, 1).reshape(sr, width)

    return pair.reshape(sr, res, -1), by_row(lg), by_row(rg), gw, gb.reshape(-1)


def streamed_local(
    left_features,
    right_features,
    alignment_mask,
    projection_weight,
    projection_bias,
    pair_output_cotangent,
):
    shard_rows, row_channel_width = left_features.shape
    alignment_depth = alignment_mask.shape[1]
    channel_count = row_channel_width // alignment_depth
    hidden_width = projection_weight.shape[0]
    pair_width = projection_weight.shape[1]
    mask_halfwidth = alignment_mask.astype(jnp.bfloat16)
    shard_mask = alignment_mask.astype(jnp.float32)
    left_masked = (
        left_features.reshape(shard_rows, alignment_depth, channel_count)
        * mask_halfwidth[:, :, None]
    )
    right_masked = (
        right_features.reshape(shard_rows, alignment_depth, channel_count)
        * mask_halfwidth[:, :, None]
    ).reshape(shard_rows, row_channel_width)
    gathered_right, gathered_mask = (
        lax.all_gather(right_masked, "row", axis=0, tiled=True),
        lax.all_gather(mask_halfwidth, "row", axis=0, tiled=True),
    )
    residues = gathered_right.shape[0]
    rows_per_block = math.gcd(residues, 128)
    number_of_blocks = residues // rows_per_block
    right_block_list = gathered_right.reshape(
        number_of_blocks, rows_per_block, alignment_depth, channel_count
    )
    mask_block_list = gathered_mask.reshape(number_of_blocks, rows_per_block, alignment_depth)
    cot_blocks = pair_output_cotangent.reshape(
        shard_rows, number_of_blocks, rows_per_block, pair_width
    ).transpose(1, 0, 2, 3)

    def block_step(state_carry, inputs):
        left_acc, weight_acc, bias_acc = state_carry
        right_blk, mask_blk, cot_blk = inputs
        counts = jnp.dot(
            shard_mask, mask_blk.astype(jnp.float32).T, precision=lax.Precision.HIGHEST
        )
        pair_norm = jnp.maximum(counts, 1.0)[:, :, None]
        outer_prod = jnp.einsum(
            "isc,jse->ijce", left_masked, right_blk, preferred_element_type=jnp.float32
        ).reshape(shard_rows, rows_per_block, hidden_width)
        prob = (outer_prod / pair_norm).astype(jnp.bfloat16)
        flat_prob = prob.reshape(shard_rows * rows_per_block, hidden_width)
        cot_flat = cot_blk.reshape(shard_rows * rows_per_block, pair_width)
        pair_block = (
            jnp.dot(flat_prob, projection_weight, preferred_element_type=jnp.float32)
            + projection_bias
        ).astype(jnp.bfloat16)
        prob_grad = lax.dot_general(
            cot_flat,
            projection_weight,
            (((1,), (1,)), ((), ())),
            preferred_element_type=jnp.float32,
        )
        outer_grad = (
            prob_grad.reshape(shard_rows, rows_per_block, hidden_width) / pair_norm
        ).astype(jnp.bfloat16)
        left_acc = left_acc + jnp.einsum(
            "ijce,jse->isc",
            outer_grad.reshape(shard_rows, rows_per_block, channel_count, channel_count),
            right_blk,
            preferred_element_type=jnp.float32,
        )
        weight_acc = weight_acc + lax.dot_general(
            flat_prob, cot_flat, (((0,), (0,)), ((), ())), preferred_element_type=jnp.float32
        )
        bias_acc = bias_acc + jnp.sum(cot_flat.astype(jnp.float32), axis=0)
        return (
            (left_acc, weight_acc, bias_acc),
            (pair_block.reshape(shard_rows, rows_per_block, pair_width), outer_grad),
        )

    starting_carry = (
        jnp.zeros((shard_rows, alignment_depth, channel_count), jnp.float32),
        jnp.zeros((hidden_width, pair_width), jnp.float32),
        jnp.zeros((pair_width,), jnp.float32),
    )
    (left_acc, weight_acc, bias_acc), (pairs, grads_out) = lax.scan(
        block_step, starting_carry, (right_block_list, mask_block_list, cot_blocks)
    )
    pair_out = pairs.transpose(1, 0, 2, 3).reshape(shard_rows, residues, pair_width)
    outer_all = grads_out.transpose(1, 0, 2, 3).reshape(
        shard_rows, residues, channel_count, channel_count
    )
    weight_sum, bias_sum = lax.psum((weight_acc, bias_acc), "row")
    left_feature_gradient = (left_acc * shard_mask[:, :, None]).reshape(
        shard_rows, row_channel_width
    )
    result = jnp.einsum("ijce,isc->jse", outer_all, left_masked, preferred_element_type=jnp.float32)
    right_accumulator = lax.psum_scatter(
        result.reshape(shard_rows * lax.axis_size("row"), row_channel_width),
        "row",
        scatter_dimension=0,
        tiled=True,
    ).reshape(shard_rows, alignment_depth, channel_count)
    right_feature_gradient = (right_accumulator * shard_mask[:, :, None]).reshape(
        shard_rows, row_channel_width
    )
    return (
        pair_out,
        left_feature_gradient,
        right_feature_gradient,
        weight_sum / residues,
        bias_sum / residues,
    )


def solution(mesh):
    in_specs = (
        P(("groups", "row"), None),
        P(("groups", "row"), None),
        P(("groups", "row"), None),
        P(),
        P(),
        P(("groups", "row"), None, None),
    )
    out_specs = (
        P(("groups", "row"), None, None),
        P(("groups", "row"), None),
        P(("groups", "row"), None),
        P("groups", None),
        P("groups"),
    )
    size = mesh.shape["row"]

    def local(left, right, mask, weight, bias, cot):
        sr, depth = mask.shape
        ch = left.shape[1] // depth
        res = sr * size
        fits = (
            size == 16 and res % 16 == 0 and res <= 64 and ch == 32 and (sr * ch) % 16 == 0
            and depth == 128 and cot.shape[2] == 128 and sr <= 16
        )
        return (gathered_local if fits else streamed_local)(left, right, mask, weight, bias, cot)

    return jax.shard_map(local, mesh=mesh, in_specs=in_specs, out_specs=out_specs, check_vma=False)
```

```python
import functools
import math

import jax
import jax.numpy as jnp
from jax import lax
from jax.experimental import pallas as pl
from jax.experimental.pallas import tpu as pltpu
from jax.sharding import PartitionSpec as P

MESH = pl.DeviceIdType.MESH
NT = (((1,), (1,)), ((), ()))
TN = (((0,), (0,)), ((), ()))


def dot(a, b, dims=(((1,), (0,)), ((), ()))):
    return lax.dot_general(a, b, dims, preferred_element_type=jnp.float32)


def fused_kernel(
    levels, n, sr, ch,
    left_ref, right_ref, mask_ref, w_ref, bias_ref, cot_ref,
    pair_ref, lg_ref, rg_ref, gw_ref, gb_ref,
    gf, gc, fa, fb, fc, mf, rn, bp, ap, wf, wl, wr, cb, t, acc, xf, m16,
    send_sem, recv_sem,
):
    f32, bf16 = jnp.float32, jnp.bfloat16
    group = lax.axis_index("groups")
    me = lax.axis_index("row")
    res, pad, lane, hp = n * sr, 64, 128, ch // 2
    fr = sr * ch
    rows = 2 * fr + 16
    q = lane // ch
    core, x, z = lax.rem(me, 2), lax.rem(me // 2, 2), me // 4
    other = 1 - x

    def rank(zz, xx, cc):
        return zz * 4 + xx * 2 + cc

    sib, xn = rank(z, x, 1 - core), rank(z, other, core)
    up, dn = rank(z + 1, x, core), rank(z - 1, x, core)
    has_up, has_dn = z < levels - 1, z > 0

    barrier = pltpu.get_barrier_semaphore()

    def greet(target):
        pl.semaphore_signal(barrier, inc=1, device_id=(group, target), device_id_type=MESH)

    greet(sib)
    greet(xn)
    pl.when(has_up)(lambda: greet(up))
    pl.when(has_dn)(lambda: greet(dn))

    m16[...] = jnp.zeros_like(m16)
    m16[:sr] = mask_ref[...].astype(f32)
    row_at = lax.broadcasted_iota(jnp.int32, (lane, lane), 0)
    lane_at = lax.broadcasted_iota(jnp.int32, (lane, lane), 1)
    order = ((row_at % q) * (lane // q) + row_at // q == lane_at).astype(bf16)
    own_mask = dot(m16[...].astype(bf16), order)
    slot = pl.multiple_of(me * rows, 16)
    gf[pl.ds(slot + 2 * fr, 16)] = own_mask.astype(bf16)
    xf[...] = jnp.zeros_like(xf)
    for side_index, ref in enumerate((left_ref, right_ref)):
        for h in range(ch):
            xf[pl.ds(h, sr, stride=ch), :] = ref[:, h * lane:(h + 1) * lane].astype(f32)
        turned = xf[...].T
        for i in range(sr):
            block = jnp.concatenate(
                [turned[u * ch:(u + 1) * ch, i * ch:(i + 1) * ch] for u in range(q)], 1
            )
            gf[pl.ds(slot + side_index * fr + i * ch, ch)] = (block * own_mask[i:i + 1]).astype(bf16)
    gc[pl.ds(pl.multiple_of(me * sr * res, 16), sr * res)] = cot_ref[...]

    pl.semaphore_wait(barrier, 2 + has_up.astype(jnp.int32) + has_dn.astype(jnp.int32))

    pending = []
    split = res
    FEATURES, COT_X, COT_Z = 0, 1, 2

    def place(owner, piece):
        if piece == FEATURES:
            return gf.at[pl.ds(pl.multiple_of(owner * rows, 16), rows)]
        first = pl.multiple_of(owner * sr * res, 16)
        if piece == COT_X:
            return gc.at[pl.ds(first, split)]
        return gc.at[pl.ds(first + split, sr * res - split)]

    def copy_of(owner, piece, target, index):
        return pltpu.make_async_remote_copy(
            src_ref=place(owner, piece),
            dst_ref=place(owner, piece),
            send_sem=send_sem.at[index],
            recv_sem=recv_sem.at[owner, piece],
            device_id=(group, target),
            device_id_type=MESH,
        )

    def guarded(cond, action):
        if cond is None:
            action()
        else:
            pl.when(cond)(action)

    def send(owner, piece, target, cond=None):
        copy = copy_of(owner, piece, target, len(pending))
        pending.append((copy, cond))
        guarded(cond, copy.start)

    def spread(owner, cond=None):
        def action():
            base = pl.multiple_of(owner * rows, 16)
            for k in range(sr):
                at = pl.ds(owner * sr + k, ch, stride=pad)
                fa[at, :] = gf[pl.ds(base + k * ch, ch)].astype(f32)
                fb[at, :] = gf[pl.ds(base + fr + k * ch, ch)].astype(f32)
            masks = gf[pl.ds(base + 2 * fr, 16)].astype(f32)
            for k in range(sr):
                mf[pl.ds(owner * sr + k, 1), :] = masks[k:k + 1]
        guarded(cond, action)

    def arrive(owner, piece, cond=None):
        guarded(cond, copy_of(owner, piece, sib, 0).wait_recv)

    def both(a, b):
        return a if b is None else jnp.logical_and(a, b)

    def start(piece):
        if piece == COT_X:
            send(me, piece, xn)
        send(me, piece, up, has_up)
        send(me, piece, dn, has_dn)
        if piece != COT_X:
            send(me, piece, xn)
        send(me, piece, sib)

    def from_level(k, sign, same_column, piece):
        zo = z + sign * k
        cond = zo >= 0 if sign < 0 else zo <= levels - 1
        owner = rank(zo, x if same_column else other, core)
        arrive(owner, piece, cond)
        if k < levels - 1 and (same_column or piece == COT_X):
            onward, has_onward = (up, has_up) if sign < 0 else (dn, has_dn)
            send(owner, piece, onward, both(has_onward, cond))
        if same_column and piece != COT_X:
            send(owner, piece, xn, cond)
        send(owner, piece, sib, cond)
        return owner, cond

    def from_x(piece):
        arrive(xn, piece)
        if piece == COT_X:
            send(xn, piece, up, has_up)
            send(xn, piece, dn, has_dn)
        send(xn, piece, sib)

    start(FEATURES)

    fa[...] = jnp.zeros_like(fa)
    fb[...] = jnp.zeros_like(fb)
    mf[...] = jnp.zeros_like(mf)
    cb[...] = jnp.zeros_like(cb)
    wf[...] = w_ref[...].astype(f32)
    spread(me)

    done = []
    for k in range(1, levels):
        for sign in (-1, 1):
            done.append(from_level(k, sign, True, FEATURES))
        if k == 1:
            from_x(FEATURES)
            done.append((xn, None))
        for sign in (-1, 1):
            done.append(from_level(k, sign, False, FEATURES))
        if k == 1:
            start(COT_X)
            start(COT_Z)
        for owner, cond in done:
            spread(owner, cond)
        done = []
        if k == 1:
            for p in range(hp):
                for h in range(2):
                    c = 2 * p + h
                    wl[p * ch:(p + 1) * ch, h * lane:(h + 1) * lane] = (
                        wf[pl.ds(c, ch, stride=ch), :].astype(bf16)
                    )
                    wr[p * ch:(p + 1) * ch, h * lane:(h + 1) * lane] = w_ref[c * ch:(c + 1) * ch]
    for zz in range(levels):
        for xx in range(2):
            owner = rank(zz, xx, 1 - core)
            arrive(owner, FEATURES)
            spread(owner)

    masks = mf[...].astype(bf16)
    rn[...] = 1.0 / jnp.maximum(dot(masks, jnp.concatenate([masks, masks], 0), NT), 1.0)
    bp[...] = fb[...].astype(bf16)

    def fill_cot(k, block):
        cb[k * lane:k * lane + res, 0:lane] = block
        cb[k * lane + pad:k * lane + pad + res, lane:2 * lane] = block

    def prob_step(v, carry):
        base = pl.multiple_of(v * (2 * rows), 16)
        features = jnp.concatenate([gf[pl.ds(base, fr)], gf[pl.ds(base + rows, fr)]], 0)
        for p in range(0, hp, 2):
            o = dot(features, bp[p * lane:(p + 2) * lane], NT)
            for k in range(2 * sr):
                scale = rn[pl.ds(v * (2 * sr) + k, 1), :]
                for u in range(2):
                    t[v, (p + u) * ch:(p + u + 1) * ch, k * lane:(k + 1) * lane] = (
                        o[k * ch:(k + 1) * ch, u * lane:(u + 1) * lane] * scale
                    ).astype(bf16)
        return carry

    def prob_steps(part):
        lax.fori_loop(part * (n // 8), (part + 1) * (n // 8), prob_step, 0)

    from_x(COT_X)
    for k in range(1, levels):
        for sign in (-1, 1):
            from_level(k, sign, True, COT_Z)
            from_level(k, sign, True, COT_X)
        prob_steps(k - 1)
        for sign in (-1, 1):
            from_level(k, sign, False, COT_X)
        if k == 1:
            from_x(COT_Z)
        for sign in (-1, 1):
            from_level(k, sign, False, COT_Z)
    prob_steps(3)
    ap[...] = fa[...].astype(bf16)

    width = sr * lane
    scales = jnp.concatenate([rn[pl.ds(me * sr + k, 1), :] for k in range(sr)], 1)

    def side(weights, features, out_ref):
        og = (dot(weights, cb[:width], NT) * scales).astype(bf16)
        flat = jnp.concatenate(
            [
                jnp.concatenate(
                    [og[p * ch:(p + 1) * ch, k * lane:(k + 1) * lane] for p in range(hp)], 1
                )
                for k in range(sr)
            ],
            0,
        )
        grad = dot(flat, features[...])
        grads = [grad[k * ch:(k + 1) * ch] * mf[pl.ds(me * sr + k, 1), :] for k in range(sr)]
        fill = [jnp.zeros((ch, lane - fr), f32)] if fr < lane else []
        turned = jnp.concatenate(
            [
                jnp.concatenate([grads[k][:, u * ch:(u + 1) * ch] for k in range(sr)] + fill, 1)
                for u in range(q)
            ],
            0,
        )
        xf[...] = turned.T
        for h in range(ch):
            out_ref[:, h * lane:(h + 1) * lane] = xf[pl.ds(h, sr, stride=ch), :]

    for k in range(sr):
        fill_cot(k, cot_ref[k * res:(k + 1) * res])
    side(wl[...], bp, lg_ref)
    features = gf[pl.ds(slot, fr)]
    for p in range(0, hp, 2):
        o = dot(features, bp[p * lane:(p + 2) * lane], NT)
        for k in range(sr):
            for u in range(2):
                acc[(p + u) * ch:(p + u + 1) * ch, k * lane:(k + 1) * lane] = (
                    o[k * ch:(k + 1) * ch, u * lane:(u + 1) * lane] * scales[:, k * lane:(k + 1) * lane]
                )
    pairs = dot(acc[...].astype(bf16), wl[...], TN)
    for k in range(sr):
        pair_ref[k * res:(k + 1) * res] = (
            pairs[k * lane:k * lane + res, :lane]
            + pairs[k * lane + pad:k * lane + pad + res, lane:]
            + bias_ref[...]
        ).astype(bf16)

    for zz in range(levels):
        for xx in range(2):
            arrive(rank(zz, xx, 1 - core), COT_X)
            arrive(rank(zz, xx, 1 - core), COT_Z)

    fc[...] = gc[...].astype(f32)
    gb_ref[...] = jnp.sum(fc[...], axis=0, keepdims=True) * (1.0 / res)
    for k in range(sr):
        fill_cot(k, fc[pl.ds(me * sr + k, res, stride=res), :].astype(bf16))
    side(wr[...], ap, rg_ref)

    acc[:, :2 * lane] = jnp.zeros((ch * hp, 2 * lane), f32)

    def weight_step(v, carry):
        first = pl.multiple_of(v * (2 * sr * res), 16)
        for k in range(2 * sr):
            fill_cot(k, gc[pl.ds(first + k * res, res)])
        acc[:, :2 * lane] += dot(t[v], cb[...])
        return carry

    lax.fori_loop(0, n // 2, weight_step, 0)
    for p in range(hp):
        for h in range(2):
            gw_ref[pl.ds(2 * p + h, ch, stride=ch), :] = (
                acc[p * ch:(p + 1) * ch, h * lane:(h + 1) * lane] * (1.0 / res)
            )
    for copy, cond in pending:
        guarded(cond, copy.wait_send)


def gathered_local(
    left_features,
    right_features,
    alignment_mask,
    projection_weight,
    projection_bias,
    pair_output_cotangent,
):
    f32, bf16 = jnp.float32, jnp.bfloat16
    sr, width = left_features.shape
    depth = alignment_mask.shape[1]
    ch = width // depth
    n = lax.axis_size("row")
    res, hidden, lane = n * sr, ch * ch, 128
    vmem = pl.BlockSpec(memory_space=pltpu.VMEM)
    pair, lg, rg, gw, gb = pl.pallas_call(
        functools.partial(fused_kernel, n // 4, n, sr, ch),
        out_shape=(
            jax.ShapeDtypeStruct((sr * res, lane), bf16),
            jax.ShapeDtypeStruct((sr, width), f32),
            jax.ShapeDtypeStruct((sr, width), f32),
            jax.ShapeDtypeStruct((hidden, lane), f32),
            jax.ShapeDtypeStruct((1, lane), f32),
        ),
        in_specs=[vmem] * 6,
        out_specs=(vmem,) * 5,
        scratch_shapes=[
            pltpu.VMEM((n * (2 * sr * ch + 16), lane), bf16),
            pltpu.VMEM((res * res, lane), bf16),
            pltpu.VMEM((ch * 64, lane), f32),
            pltpu.VMEM((ch * 64, lane), f32),
            pltpu.VMEM((res * res, lane), f32),
            pltpu.VMEM((64, lane), f32),
            pltpu.VMEM((64, lane), f32),
            pltpu.VMEM((ch * 64, lane), bf16),
            pltpu.VMEM((ch * 64, lane), bf16),
            pltpu.VMEM((hidden, lane), f32),
            pltpu.VMEM((hidden // 2, 2 * lane), bf16),
            pltpu.VMEM((hidden // 2, 2 * lane), bf16),
            pltpu.VMEM((2 * sr * lane, 2 * lane), bf16),
            pltpu.VMEM((n // 2, hidden // 2, 2 * sr * lane), bf16),
            pltpu.VMEM((hidden // 2, max(sr, 2) * lane), f32),
            pltpu.VMEM((lane, lane), f32),
            pltpu.VMEM((16, lane), f32),
            pltpu.SemaphoreType.DMA((96,)),
            pltpu.SemaphoreType.DMA((n, 3)),
        ],
        compiler_params=pltpu.CompilerParams(
            collective_id=0, has_side_effects=True, vmem_limit_bytes=48 * 1024 * 1024
        ),
        name="fused",
    )(
        left_features,
        right_features,
        alignment_mask,
        projection_weight,
        projection_bias.reshape(1, -1),
        pair_output_cotangent.reshape(sr * res, -1),
    )
    return pair.reshape(sr, res, -1), lg, rg, gw, gb.reshape(-1)


def streamed_local(
    left_features,
    right_features,
    alignment_mask,
    projection_weight,
    projection_bias,
    pair_output_cotangent,
):
    shard_rows, row_channel_width = left_features.shape
    alignment_depth = alignment_mask.shape[1]
    channel_count = row_channel_width // alignment_depth
    hidden_width = projection_weight.shape[0]
    pair_width = projection_weight.shape[1]
    mask_halfwidth = alignment_mask.astype(jnp.bfloat16)
    shard_mask = alignment_mask.astype(jnp.float32)
    left_masked = (
        left_features.reshape(shard_rows, alignment_depth, channel_count)
        * mask_halfwidth[:, :, None]
    )
    right_masked = (
        right_features.reshape(shard_rows, alignment_depth, channel_count)
        * mask_halfwidth[:, :, None]
    ).reshape(shard_rows, row_channel_width)
    gathered_right, gathered_mask = (
        lax.all_gather(right_masked, "row", axis=0, tiled=True),
        lax.all_gather(mask_halfwidth, "row", axis=0, tiled=True),
    )
    residues = gathered_right.shape[0]
    rows_per_block = math.gcd(residues, 128)
    number_of_blocks = residues // rows_per_block
    right_block_list = gathered_right.reshape(
        number_of_blocks, rows_per_block, alignment_depth, channel_count
    )
    mask_block_list = gathered_mask.reshape(number_of_blocks, rows_per_block, alignment_depth)
    cot_blocks = pair_output_cotangent.reshape(
        shard_rows, number_of_blocks, rows_per_block, pair_width
    ).transpose(1, 0, 2, 3)

    def block_step(state_carry, inputs):
        left_acc, weight_acc, bias_acc = state_carry
        right_blk, mask_blk, cot_blk = inputs
        counts = jnp.dot(
            shard_mask, mask_blk.astype(jnp.float32).T, precision=lax.Precision.HIGHEST
        )
        pair_norm = jnp.maximum(counts, 1.0)[:, :, None]
        outer_prod = jnp.einsum(
            "isc,jse->ijce", left_masked, right_blk, preferred_element_type=jnp.float32
        ).reshape(shard_rows, rows_per_block, hidden_width)
        prob = (outer_prod / pair_norm).astype(jnp.bfloat16)
        flat_prob = prob.reshape(shard_rows * rows_per_block, hidden_width)
        cot_flat = cot_blk.reshape(shard_rows * rows_per_block, pair_width)
        pair_block = (
            jnp.dot(flat_prob, projection_weight, preferred_element_type=jnp.float32)
            + projection_bias
        ).astype(jnp.bfloat16)
        prob_grad = lax.dot_general(
            cot_flat,
            projection_weight,
            (((1,), (1,)), ((), ())),
            preferred_element_type=jnp.float32,
        )
        outer_grad = (
            prob_grad.reshape(shard_rows, rows_per_block, hidden_width) / pair_norm
        ).astype(jnp.bfloat16)
        left_acc = left_acc + jnp.einsum(
            "ijce,jse->isc",
            outer_grad.reshape(shard_rows, rows_per_block, channel_count, channel_count),
            right_blk,
            preferred_element_type=jnp.float32,
        )
        weight_acc = weight_acc + lax.dot_general(
            flat_prob, cot_flat, (((0,), (0,)), ((), ())), preferred_element_type=jnp.float32
        )
        bias_acc = bias_acc + jnp.sum(cot_flat.astype(jnp.float32), axis=0)
        return (
            (left_acc, weight_acc, bias_acc),
            (pair_block.reshape(shard_rows, rows_per_block, pair_width), outer_grad),
        )

    starting_carry = (
        jnp.zeros((shard_rows, alignment_depth, channel_count), jnp.float32),
        jnp.zeros((hidden_width, pair_width), jnp.float32),
        jnp.zeros((pair_width,), jnp.float32),
    )
    (left_acc, weight_acc, bias_acc), (pairs, grads_out) = lax.scan(
        block_step, starting_carry, (right_block_list, mask_block_list, cot_blocks)
    )
    pair_out = pairs.transpose(1, 0, 2, 3).reshape(shard_rows, residues, pair_width)
    outer_all = grads_out.transpose(1, 0, 2, 3).reshape(
        shard_rows, residues, channel_count, channel_count
    )
    weight_sum, bias_sum = lax.psum((weight_acc, bias_acc), "row")
    left_feature_gradient = (left_acc * shard_mask[:, :, None]).reshape(
        shard_rows, row_channel_width
    )
    result = jnp.einsum("ijce,isc->jse", outer_all, left_masked, preferred_element_type=jnp.float32)
    right_accumulator = lax.psum_scatter(
        result.reshape(shard_rows * lax.axis_size("row"), row_channel_width),
        "row",
        scatter_dimension=0,
        tiled=True,
    ).reshape(shard_rows, alignment_depth, channel_count)
    right_feature_gradient = (right_accumulator * shard_mask[:, :, None]).reshape(
        shard_rows, row_channel_width
    )
    return (
        pair_out,
        left_feature_gradient,
        right_feature_gradient,
        weight_sum / residues,
        bias_sum / residues,
    )


def solution(mesh):
    in_specs = (
        P(("groups", "row"), None),
        P(("groups", "row"), None),
        P(("groups", "row"), None),
        P(),
        P(),
        P(("groups", "row"), None, None),
    )
    out_specs = (
        P(("groups", "row"), None, None),
        P(("groups", "row"), None),
        P(("groups", "row"), None),
        P("groups", None),
        P("groups"),
    )
    size = mesh.shape["row"]

    def local(left, right, mask, weight, bias, cot):
        sr, depth = mask.shape
        ch = left.shape[1] // depth
        res = sr * size
        fits = (
            size == 16 and res % 16 == 0 and res <= 64 and ch == 32 and (sr * ch) % 16 == 0 and 2 <= sr <= 4
            and depth == 128 and cot.shape[2] == 128
        )
        return (gathered_local if fits else streamed_local)(left, right, mask, weight, bias, cot)

    return jax.shard_map(local, mesh=mesh, in_specs=in_specs, out_specs=out_specs, check_vma=False)
```

```python
import functools
import math

import jax
import jax.numpy as jnp
from jax import lax
from jax.experimental import pallas as pl
from jax.experimental.pallas import tpu as pltpu
from jax.sharding import PartitionSpec as P

MESH = pl.DeviceIdType.MESH
NT = (((1,), (1,)), ((), ()))
TN = (((0,), (0,)), ((), ()))


def gather_kernel(
    levels, sr, ch, left_hbm, right_hbm, mask_hbm, cot_hbm, out_ref,
    left_ref, right_ref, mask_ref, xf, m16, send_sem, recv_sem, own_sem,
):
    f32, bf16 = jnp.float32, jnp.bfloat16
    lane, q = 128, 128 // ch
    fr = sr * ch
    cot_rows = cot_hbm.shape[0]
    rows = out_ref.shape[0] // (levels * 4)
    loads = [
        pltpu.make_async_copy(source, target, own_sem.at[k])
        for k, (source, target) in enumerate(
            ((left_hbm, left_ref), (right_hbm, right_ref), (mask_hbm, mask_ref))
        )
    ]
    group = lax.axis_index("groups")
    me = lax.axis_index("row")
    core = lax.rem(me, 2)
    x = lax.rem(me // 2, 2)
    z = me // 4

    def rank(zz, xx, cc):
        return zz * 4 + xx * 2 + cc

    sib, xn = rank(z, x, 1 - core), rank(z, 1 - x, core)
    up, dn = rank(z + 1, x, core), rank(z - 1, x, core)
    has_up, has_dn = z < levels - 1, z > 0

    barrier = pltpu.get_barrier_semaphore()

    def greet(target):
        pl.semaphore_signal(barrier, inc=1, device_id=(group, target), device_id_type=MESH)

    greet(sib)
    greet(xn)
    pl.when(has_up)(lambda: greet(up))
    pl.when(has_dn)(lambda: greet(dn))
    slot = pl.multiple_of(me * rows, 16)
    cot_copy = pltpu.make_async_copy(
        cot_hbm, out_ref.at[pl.ds(slot + 2 * fr, cot_rows)], own_sem.at[3]
    )
    for load in loads:
        load.start()
    cot_copy.start()

    m16[...] = jnp.zeros_like(m16)
    xf[...] = jnp.zeros_like(xf)
    for load in loads:
        load.wait()
    m16[:sr] = mask_ref[...].astype(f32)
    row_at = lax.broadcasted_iota(jnp.int32, (lane, lane), 0)
    lane_at = lax.broadcasted_iota(jnp.int32, (lane, lane), 1)
    order = ((row_at % q) * (lane // q) + row_at // q == lane_at).astype(bf16)
    own_mask = jnp.dot(m16[...].astype(bf16), order, preferred_element_type=f32)
    out_ref[pl.ds(slot + 2 * fr + cot_rows, 16)] = own_mask.astype(bf16)
    for side_index, ref in enumerate((left_ref, right_ref)):
        for h in range(ch):
            xf[pl.ds(h, sr, stride=ch), :] = ref[:, h * lane:(h + 1) * lane].astype(f32)
        turned = xf[...].T
        for i in range(sr):
            block = jnp.concatenate(
                [turned[u * ch:(u + 1) * ch, i * ch:(i + 1) * ch] for u in range(q)], 1
            )
            out_ref[pl.ds(slot + side_index * fr + i * ch, ch)] = (block * own_mask[i:i + 1]).astype(bf16)
    tail = slot + 2 * fr + cot_rows + 16
    spare = rows - 2 * fr - cot_rows - 16
    if spare:
        out_ref[pl.ds(tail, spare)] = jnp.zeros((spare, lane), bf16)
    cot_copy.wait()

    pl.semaphore_wait(barrier, 2 + has_up.astype(jnp.int32) + has_dn.astype(jnp.int32))

    pending = []
    cut = rows // 6 // 16 * 16
    mid = (rows - cut) // 2 // 16 * 16

    def place(owner, half):
        first, count = ((0, cut), (cut, mid), (cut + mid, rows - cut - mid))[half]
        return out_ref.at[pl.ds(pl.multiple_of(owner * rows + first, 16), count)]

    def copy_of(owner, half, target, index):
        src = place(owner, half)
        return pltpu.make_async_remote_copy(
            src_ref=src,
            dst_ref=place(owner, half),
            send_sem=send_sem.at[index],
            recv_sem=recv_sem.at[owner, half],
            device_id=(group, target),
            device_id_type=MESH,
        )

    def send(owner, half, target, cond=None):
        copy = copy_of(owner, half, target, len(pending))
        pending.append((copy, cond))
        if cond is None:
            copy.start()
        else:
            pl.when(cond)(copy.start)

    def arrive(owner, half, cond=None):
        copy = copy_of(owner, half, sib, 0)
        if cond is None:
            copy.wait_recv()
        else:
            pl.when(cond)(copy.wait_recv)

    def both(a, b):
        return a if b is None else jnp.logical_and(a, b)

    send(me, 0, xn)
    for piece in (1, 2):
        send(me, piece, up, has_up)
        send(me, piece, dn, has_dn)
        send(me, piece, xn)
    send(me, 0, up, has_up)
    send(me, 0, dn, has_dn)
    for piece in (1, 2, 0):
        send(me, piece, sib)

    arrive(xn, 0)
    send(xn, 0, up, has_up)
    send(xn, 0, dn, has_dn)
    send(xn, 0, sib)

    def from_level(k, sign, xx, half):
        zo = z + sign * k
        cond = zo >= 0 if sign < 0 else zo <= levels - 1
        owner = rank(zo, xx, core)
        arrive(owner, half, cond)
        if half == 0 or xx is x:
            onward, has_onward = (up, has_up) if sign < 0 else (dn, has_dn)
            if k < levels - 1:
                send(owner, half, onward, both(has_onward, cond))
        if half != 0 and xx is x:
            send(owner, half, xn, cond)
        send(owner, half, sib, cond)

    other = 1 - x
    for k in range(1, levels):
        for piece in (1, 2, 0):
            for sign in (-1, 1):
                from_level(k, sign, x, piece)
        if k == 1:
            for piece in (1, 2):
                arrive(xn, piece)
                send(xn, piece, sib)
        for piece in (0, 1, 2):
            for sign in (-1, 1):
                from_level(k, sign, other, piece)

    for zz in range(levels):
        for xx in range(2):
            for piece in range(3):
                arrive(rank(zz, xx, 1 - core), piece)
    for copy, cond in pending:
        if cond is None:
            copy.wait_send()
        else:
            pl.when(cond)(copy.wait_send)


def gather(left, right, mask, cot, size, sr, ch, rows):
    lane = cot.shape[1]
    any_space = pl.BlockSpec(memory_space=pl.ANY)
    return pl.pallas_call(
        functools.partial(gather_kernel, size // 4, sr, ch),
        out_shape=jax.ShapeDtypeStruct((size * rows, lane), cot.dtype),
        in_specs=[any_space] * 4,
        out_specs=pl.BlockSpec(memory_space=pltpu.VMEM),
        scratch_shapes=[
            pltpu.VMEM(left.shape, left.dtype),
            pltpu.VMEM(right.shape, right.dtype),
            pltpu.VMEM(mask.shape, mask.dtype),
            pltpu.VMEM((lane, lane), jnp.float32),
            pltpu.VMEM((16, lane), jnp.float32),
            pltpu.SemaphoreType.DMA((128,)),
            pltpu.SemaphoreType.DMA((size, 3)),
            pltpu.SemaphoreType.DMA((4,)),
        ],
        compiler_params=pltpu.CompilerParams(
            collective_id=0, has_side_effects=True, vmem_limit_bytes=32 * 1024 * 1024
        ),
        name="gather",
    )(left, right, mask, cot)


def compute_kernel(
    n, sr, ch, rows, g, w_ref, bias_ref, pair_ref, lg_ref, rg_ref, gw_ref, gb_ref,
    fa, fb, fc, mf, rn, bp, ap, wf, wl, wr, cb, t, acc, xf,
):
    f32, bf16 = jnp.float32, jnp.bfloat16
    me = lax.axis_index("row")
    res = n * sr
    pad = 64
    lane = 128
    q = lane // ch
    hp = ch // 2
    fr = sr * ch
    cot_at, mask_at = 2 * fr, 2 * fr + sr * res

    def dot(a, b, dims=(((1,), (0,)), ((), ()))):
        return lax.dot_general(a, b, dims, preferred_element_type=f32)

    mf[...] = jnp.zeros_like(mf)
    for d in range(n):
        base = d * rows
        fa[d * fr:(d + 1) * fr] = g[base:base + fr].astype(f32)
        fb[d * fr:(d + 1) * fr] = g[base + fr:base + 2 * fr].astype(f32)
        fc[d * sr * res:(d + 1) * sr * res] = g[base + cot_at:base + mask_at].astype(f32)
        m = g[base + mask_at:base + mask_at + 16].astype(f32)[:sr]
        mf[d * sr:(d + 1) * sr] = m
    masks = mf[...].astype(bf16)
    rn[...] = 1.0 / jnp.maximum(dot(masks, jnp.concatenate([masks, masks], 0), NT), 1.0)

    bp[...] = jnp.zeros_like(bp)
    ap[...] = jnp.zeros_like(ap)
    for e in range(ch):
        bp[e * pad:e * pad + res] = fb[pl.ds(e, res, stride=ch), :].astype(bf16)
        ap[e * pad:e * pad + res] = fa[pl.ds(e, res, stride=ch), :].astype(bf16)
    wf[...] = w_ref[...].astype(f32)
    for p in range(hp):
        for h in range(2):
            c = 2 * p + h
            wl[p * ch:(p + 1) * ch, h * lane:(h + 1) * lane] = wf[pl.ds(c, ch, stride=ch), :].astype(bf16)
            wr[p * ch:(p + 1) * ch, h * lane:(h + 1) * lane] = w_ref[c * ch:(c + 1) * ch]

    gb_ref[...] = jnp.sum(fc[...], axis=0, keepdims=True) * (1.0 / res)
    cb[...] = jnp.zeros_like(cb)
    acc[...] = jnp.zeros_like(acc)

    def fill_cot(k, block):
        cb[k * lane:k * lane + res, 0:lane] = block
        cb[k * lane + pad:k * lane + pad + res, lane:2 * lane] = block

    def fill_prob(left, first, count):
        for p in range(0, hp, 2):
            o = dot(left, bp[p * lane:(p + 2) * lane], NT)
            for k in range(count):
                scale = rn[pl.ds(first + k, 1), :]
                for u in range(2):
                    t[(p + u) * ch:(p + u + 1) * ch, k * lane:(k + 1) * lane] = (
                        o[k * ch:(k + 1) * ch, u * lane:(u + 1) * lane] * scale
                    ).astype(bf16)

    def step(v, carry):
        base = pl.multiple_of(v * (2 * rows), 16)
        left = jnp.concatenate([g[pl.ds(base, fr)], g[pl.ds(base + rows, fr)]], 0)
        fill_prob(left, v * (2 * sr), 2 * sr)
        for k in range(2 * sr):
            fill_cot(k, g[pl.ds(base + (k // sr) * rows + cot_at + (k % sr) * res, res)])
        acc[...] += dot(t[...], cb[...])
        return carry

    lax.fori_loop(0, n // 2, step, 0)
    for p in range(hp):
        for h in range(2):
            gw_ref[pl.ds(2 * p + h, ch, stride=ch), :] = (
                acc[p * ch:(p + 1) * ch, h * lane:(h + 1) * lane] * (1.0 / res)
            )

    base = pl.multiple_of(me * rows, 16)
    width = sr * lane
    scales = jnp.concatenate([rn[pl.ds(me * sr + k, 1), :] for k in range(sr)], 1)

    def side(weights, features, out_ref):
        og = (dot(weights, cb[:width], NT) * scales).astype(bf16)
        flat = jnp.concatenate(
            [
                jnp.concatenate(
                    [og[p * ch:(p + 1) * ch, k * lane:(k + 1) * lane] for p in range(hp)], 1
                )
                for k in range(sr)
            ],
            0,
        )
        grad = dot(flat, features[...])
        grads = [grad[k * ch:(k + 1) * ch] * mf[pl.ds(me * sr + k, 1), :] for k in range(sr)]
        fill = [jnp.zeros((ch, lane - fr), f32)] if fr < lane else []
        turned = jnp.concatenate(
            [
                jnp.concatenate([grads[k][:, u * ch:(u + 1) * ch] for k in range(sr)] + fill, 1)
                for u in range(q)
            ],
            0,
        )
        xf[...] = turned.T
        for h in range(ch):
            out_ref[:, h * lane:(h + 1) * lane] = xf[pl.ds(h, sr, stride=ch), :]

    fill_prob(g[pl.ds(base, fr)], me * sr, sr)
    for k in range(sr):
        fill_cot(k, g[pl.ds(base + cot_at + k * res, res)])
    pairs = dot(t[:, :width], wl[...], TN)
    side(wl[...], bp, lg_ref)
    for k in range(sr):
        pair_ref[k * res:(k + 1) * res] = (
            pairs[k * lane:k * lane + res, :lane]
            + pairs[k * lane + pad:k * lane + pad + res, lane:]
            + bias_ref[...]
        ).astype(bf16)
    for k in range(sr):
        fill_cot(k, fc[pl.ds(me * sr + k, res, stride=res), :].astype(bf16))
    side(wr[...], ap, rg_ref)


def compute(g, weight, bias, n, sr, ch, rows):
    f32, bf16 = jnp.float32, jnp.bfloat16
    res, hidden, lane = n * sr, ch * ch, 128
    vmem = pl.BlockSpec(memory_space=pltpu.VMEM)
    return pl.pallas_call(
        functools.partial(compute_kernel, n, sr, ch, rows),
        out_shape=(
            jax.ShapeDtypeStruct((sr * res, lane), bf16),
            jax.ShapeDtypeStruct((sr, ch * lane), f32),
            jax.ShapeDtypeStruct((sr, ch * lane), f32),
            jax.ShapeDtypeStruct((hidden, lane), f32),
            jax.ShapeDtypeStruct((1, lane), f32),
        ),
        in_specs=[vmem] * 3,
        out_specs=(vmem,) * 5,
        scratch_shapes=[
            pltpu.VMEM((res * ch, lane), f32),
            pltpu.VMEM((res * ch, lane), f32),
            pltpu.VMEM((res * res, lane), f32),
            pltpu.VMEM((64, lane), f32),
            pltpu.VMEM((64, lane), f32),
            pltpu.VMEM((ch * 64, lane), bf16),
            pltpu.VMEM((ch * 64, lane), bf16),
            pltpu.VMEM((hidden, lane), f32),
            pltpu.VMEM((hidden // 2, 2 * lane), bf16),
            pltpu.VMEM((hidden // 2, 2 * lane), bf16),
            pltpu.VMEM((2 * sr * lane, 2 * lane), bf16),
            pltpu.VMEM((hidden // 2, 2 * sr * lane), bf16),
            pltpu.VMEM((hidden // 2, 2 * lane), f32),
            pltpu.VMEM((lane, lane), f32),
        ],
        compiler_params=pltpu.CompilerParams(vmem_limit_bytes=40 * 1024 * 1024),
        name="compute",
    )(g, weight, bias)


def gathered_local(
    left_features,
    right_features,
    alignment_mask,
    projection_weight,
    projection_bias,
    pair_output_cotangent,
):
    sr, width = left_features.shape
    depth = alignment_mask.shape[1]
    ch = width // depth
    n = lax.axis_size("row")
    res = n * sr
    rows = -(-(2 * sr * ch + sr * res + 16) // 32) * 32
    gathered = gather(
        left_features, right_features, alignment_mask,
        pair_output_cotangent.reshape(sr * res, -1), n, sr, ch, rows,
    )
    pair, lg, rg, gw, gb = compute(
        gathered, projection_weight, projection_bias.reshape(1, -1), n, sr, ch, rows
    )
    return pair.reshape(sr, res, -1), lg, rg, gw, gb.reshape(-1)


def streamed_local(
    left_features,
    right_features,
    alignment_mask,
    projection_weight,
    projection_bias,
    pair_output_cotangent,
):
    shard_rows, row_channel_width = left_features.shape
    alignment_depth = alignment_mask.shape[1]
    channel_count = row_channel_width // alignment_depth
    hidden_width = projection_weight.shape[0]
    pair_width = projection_weight.shape[1]
    mask_halfwidth = alignment_mask.astype(jnp.bfloat16)
    shard_mask = alignment_mask.astype(jnp.float32)
    left_masked = (
        left_features.reshape(shard_rows, alignment_depth, channel_count)
        * mask_halfwidth[:, :, None]
    )
    right_masked = (
        right_features.reshape(shard_rows, alignment_depth, channel_count)
        * mask_halfwidth[:, :, None]
    ).reshape(shard_rows, row_channel_width)
    gathered_right, gathered_mask = (
        lax.all_gather(right_masked, "row", axis=0, tiled=True),
        lax.all_gather(mask_halfwidth, "row", axis=0, tiled=True),
    )
    residues = gathered_right.shape[0]
    rows_per_block = math.gcd(residues, 128)
    number_of_blocks = residues // rows_per_block
    right_block_list = gathered_right.reshape(
        number_of_blocks, rows_per_block, alignment_depth, channel_count
    )
    mask_block_list = gathered_mask.reshape(number_of_blocks, rows_per_block, alignment_depth)
    cot_blocks = pair_output_cotangent.reshape(
        shard_rows, number_of_blocks, rows_per_block, pair_width
    ).transpose(1, 0, 2, 3)

    def block_step(state_carry, inputs):
        left_acc, weight_acc, bias_acc = state_carry
        right_blk, mask_blk, cot_blk = inputs
        counts = jnp.dot(
            shard_mask, mask_blk.astype(jnp.float32).T, precision=lax.Precision.HIGHEST
        )
        pair_norm = jnp.maximum(counts, 1.0)[:, :, None]
        outer_prod = jnp.einsum(
            "isc,jse->ijce", left_masked, right_blk, preferred_element_type=jnp.float32
        ).reshape(shard_rows, rows_per_block, hidden_width)
        prob = (outer_prod / pair_norm).astype(jnp.bfloat16)
        flat_prob = prob.reshape(shard_rows * rows_per_block, hidden_width)
        cot_flat = cot_blk.reshape(shard_rows * rows_per_block, pair_width)
        pair_block = (
            jnp.dot(flat_prob, projection_weight, preferred_element_type=jnp.float32)
            + projection_bias
        ).astype(jnp.bfloat16)
        prob_grad = lax.dot_general(
            cot_flat,
            projection_weight,
            (((1,), (1,)), ((), ())),
            preferred_element_type=jnp.float32,
        )
        outer_grad = (
            prob_grad.reshape(shard_rows, rows_per_block, hidden_width) / pair_norm
        ).astype(jnp.bfloat16)
        left_acc = left_acc + jnp.einsum(
            "ijce,jse->isc",
            outer_grad.reshape(shard_rows, rows_per_block, channel_count, channel_count),
            right_blk,
            preferred_element_type=jnp.float32,
        )
        weight_acc = weight_acc + lax.dot_general(
            flat_prob, cot_flat, (((0,), (0,)), ((), ())), preferred_element_type=jnp.float32
        )
        bias_acc = bias_acc + jnp.sum(cot_flat.astype(jnp.float32), axis=0)
        return (
            (left_acc, weight_acc, bias_acc),
            (pair_block.reshape(shard_rows, rows_per_block, pair_width), outer_grad),
        )

    starting_carry = (
        jnp.zeros((shard_rows, alignment_depth, channel_count), jnp.float32),
        jnp.zeros((hidden_width, pair_width), jnp.float32),
        jnp.zeros((pair_width,), jnp.float32),
    )
    (left_acc, weight_acc, bias_acc), (pairs, grads_out) = lax.scan(
        block_step, starting_carry, (right_block_list, mask_block_list, cot_blocks)
    )
    pair_out = pairs.transpose(1, 0, 2, 3).reshape(shard_rows, residues, pair_width)
    outer_all = grads_out.transpose(1, 0, 2, 3).reshape(
        shard_rows, residues, channel_count, channel_count
    )
    weight_sum, bias_sum = lax.psum((weight_acc, bias_acc), "row")
    left_feature_gradient = (left_acc * shard_mask[:, :, None]).reshape(
        shard_rows, row_channel_width
    )
    result = jnp.einsum("ijce,isc->jse", outer_all, left_masked, preferred_element_type=jnp.float32)
    right_accumulator = lax.psum_scatter(
        result.reshape(shard_rows * lax.axis_size("row"), row_channel_width),
        "row",
        scatter_dimension=0,
        tiled=True,
    ).reshape(shard_rows, alignment_depth, channel_count)
    right_feature_gradient = (right_accumulator * shard_mask[:, :, None]).reshape(
        shard_rows, row_channel_width
    )
    return (
        pair_out,
        left_feature_gradient,
        right_feature_gradient,
        weight_sum / residues,
        bias_sum / residues,
    )


def solution(mesh):
    in_specs = (
        P(("groups", "row"), None),
        P(("groups", "row"), None),
        P(("groups", "row"), None),
        P(),
        P(),
        P(("groups", "row"), None, None),
    )
    out_specs = (
        P(("groups", "row"), None, None),
        P(("groups", "row"), None),
        P(("groups", "row"), None),
        P("groups", None),
        P("groups"),
    )
    size = mesh.shape["row"]

    def local(left, right, mask, weight, bias, cot):
        sr, depth = mask.shape
        ch = left.shape[1] // depth
        res = sr * size
        fits = (
            size == 16 and res % 16 == 0 and res <= 64 and ch == 32 and (sr * ch) % 16 == 0
            and depth == 128 and cot.shape[2] == 128 and sr <= 4
        )
        return (gathered_local if fits else streamed_local)(left, right, mask, weight, bias, cot)

    return jax.shard_map(local, mesh=mesh, in_specs=in_specs, out_specs=out_specs, check_vma=False)
```
